32 devices in a mesh: ctx: 2 (over y), exp: 16 (over z, x, core).
Axes of the slice: x: 2, y: 2, z: 4, core: 2. Of those that a mesh axis runs over, the one named last changes fastest.
Arguments:
- inputs: bfloat16 [1536, 1024], P('exp', 'ctx'), may hold values from -6 to 6
- pre_act: bfloat16 [1536, 1024], P('exp', 'ctx'), may hold values from -6 to 6
- grad_out: bfloat16 [1536, 1024], P('exp', 'ctx'), may hold values from -6 to 6
- conv_weight: bfloat16 [5, 1536, 1536], P(None, 'exp', 'ctx'), may hold values from -0.0625 to 0.0625
- expert_ids: int32 [1024, 2], P('ctx'), may hold values from 0 to 15, as said below
- gate_values: float32 [1024, 2], P('ctx'), may hold values from 0.1 to 0.9
- expert_in: bfloat16 [16, 1536, 3072], P('exp', None, 'ctx'), may hold values from -0.15625 to 0.15625
- expert_out: bfloat16 [16, 3072, 1536], P('exp', 'ctx'), may hold values from -0.109375 to 0.109375
Outputs:
- grad_inputs: bfloat16 [1536, 1024], P('exp', 'ctx')
- grad_conv: float32 [5, 1536, 1536], P(None, 'exp', 'ctx')
- grad_expert_in: bfloat16 [16, 1536, 3072], P('exp', None, 'ctx')
- grad_expert_out: bfloat16 [16, 3072, 1536], P('exp', 'ctx')
The draws below stay inside these ranges and needn't reach their ends.
Inputs may be any that keep to these rules, and one draw needn't show every extreme that they name: `expert_ids`: the 2 ids of a bin differ. In each aligned block of 512 bins (the bins of one index of ctx) no expert is named more than 128 times, and one expert, the same in every block, is named exactly 128 times in each block.
All inputs are finite; a program needn't handle non-finite values.
Results may differ from the reference program's by a relative error of at most 0.009.
Values may be sent and summed in bfloat16 or wider, within the bound.
A program may use at most 128 MiB of HBM per device.

```python
import jax
import jax.numpy as jnp
from jax import lax

D = 1536
FF = 3072
KERNEL = 5
TOP = 2
BIN_CTX = 512
EXPERTS = 16
BINS = 1024
CAP = 128
N_CTX = 2


def draw_expert_ids(key, part):
    middle = CAP // 2
    hot_key = jax.random.fold_in(key, 11)
    hottest = jax.random.randint(hot_key, (), 0, EXPERTS, dtype=jnp.int32)
    positions = jnp.arange(EXPERTS, dtype=jnp.int32)

    def one_block(block_id):
        block_key = jax.random.fold_in(key, 100 + block_id)
        subkeys = jax.random.split(block_key, 4)
        scores = jax.random.randint(subkeys[0], (EXPERTS,), 1, 1 << 20, dtype=jnp.int32) * EXPERTS + positions
        scores = jnp.where(positions == hottest, 0, scores)
        ranking = jnp.argsort(scores).astype(jnp.int32)
        deltas = jax.random.randint(subkeys[1], (EXPERTS // 2,), 0, middle + 1, dtype=jnp.int32)
        signed = jnp.stack([deltas, -deltas], axis=1).reshape(-1)
        counts = (middle + signed).at[0].set(CAP).at[1].set(0)
        labels = jnp.repeat(ranking, counts, total_repeat_length=TOP * BIN_CTX)
        paired = jnp.stack([labels[:BIN_CTX], labels[BIN_CTX:]], axis=1)
        shuffled = paired[jax.random.permutation(subkeys[2], BIN_CTX)]
        swapped = jax.random.randint(subkeys[3], (BIN_CTX, 1), 0, 2, dtype=jnp.int32)
        return jnp.where(swapped == 1, shuffled[:, ::-1], shuffled)
    return lax.map(one_block, jnp.arange(N_CTX, dtype=jnp.int32)).reshape(BINS, TOP)


def steps_of(rng, extent, cuts, low, high):
    loudness = 1.0
    for dim, shards_of in cuts:
        draws = jax.random.uniform(jax.random.fold_in(jax.random.fold_in(rng, 6), dim), (shards_of,), jnp.float32, low / len(cuts), high / len(cuts))
        loudness = loudness * jnp.repeat(jnp.exp(draws), extent[dim] // shards_of).reshape((-1,) + (1,) * (len(extent) - 1 - dim))
    return loudness


def scatter_about(key, shape, width, reach, cuts=(), held_as=jnp.bfloat16):
    result = jax.random.normal(key, shape, jnp.float32) * width
    if len(cuts) > 0:
        result = steps_of(key, shape, cuts, -0.22, 0.18) * result
    return jnp.clip(result, min=-reach, max=reach).astype(held_as)


def setup_inputs(seed: int = 0) -> dict:
    splits = jax.random.split(jax.random.key(seed), 9)
    inputs = scatter_about(splits[0], (D, BINS), 1.0, 6.0, ((0, 16), (1, 2)))
    pre_act = scatter_about(splits[1], (D, BINS), 1.0, 6.0, ((0, 16), (1, 2)))
    grad_out = scatter_about(splits[2], (D, BINS), 1.0, 6.0, ((0, 16), (1, 2)))
    conv_weight = scatter_about(splits[3], (KERNEL, D, D), (KERNEL * D) ** -0.5, 0.0625, ((1, 16), (2, 2)))
    expert_ids = draw_expert_ids(jax.random.fold_in(splits[8], 71), 0)
    gate_values = jnp.clip(0.1 + 0.79999997 * jax.random.uniform(splits[5], (BINS, TOP), jnp.float32) ** steps_of(splits[5], (BINS, TOP), ((0, 2),), -0.2, 0.2), 0.1, 0.9)
    expert_in = scatter_about(splits[6], (EXPERTS, D, FF), D ** -0.5, 0.15625, ((0, 16), (2, 2)))
    expert_out = scatter_about(splits[7], (EXPERTS, FF, D), FF ** -0.5, 0.109375, ((0, 16), (1, 2)))
    return dict(inputs=inputs, pre_act=pre_act, grad_out=grad_out, conv_weight=conv_weight, expert_ids=expert_ids, gate_values=gate_values, expert_in=expert_in, expert_out=expert_out)


def gelu_value(values):
    factor = 0.7978845608028654
    return 0.5 * values * (1.0 + jnp.tanh(factor * (values + 0.044715 * values * values * values)))


def gelu_slope(values):
    factor = 0.7978845608028654
    tangent = jnp.tanh(factor * (values + 0.044715 * values * values * values))
    return 0.5 * (1.0 + tangent) + 0.5 * values * (1.0 - tangent * tangent) * factor * (1.0 + 0.134145 * values * values)


def product(left, right, dims):
    return lax.dot_general(left.astype(jnp.float32), right.astype(jnp.float32), (dims, ((), ())), precision=lax.Precision.HIGHEST, preferred_element_type=jnp.float32)


def expert_pass(w_first, w_second, rows_in, rows_grad):
    hidden = product(w_first, rows_in, ((0,), (0,)))
    squashed = gelu_value(hidden).astype(jnp.bfloat16)
    grad_second = product(squashed, rows_grad, ((1,), (1,)))
    grad_hidden = product(w_second, rows_grad, ((1,), (0,)))
    grad_pre = (grad_hidden * gelu_slope(hidden)).astype(jnp.bfloat16)
    grad_first = product(rows_in, grad_pre, ((1,), (1,)))
    grad_rows = product(w_first, grad_pre, ((1,), (0,)))
    return grad_first, grad_second, grad_rows


def reference(inputs, pre_act, grad_out, conv_weight, expert_ids, gate_values, expert_in, expert_out):
    pre_float = pre_act.astype(jnp.float32)
    activated = (inputs.astype(jnp.float32) + gelu_value(pre_float)).astype(jnp.bfloat16)
    grad_float = grad_out.astype(jnp.float32)
    rows_all = N_CTX * CAP
    flat_ids = expert_ids.reshape(N_CTX, TOP * BIN_CTX)
    onehot = (flat_ids[:, :, None] == jnp.arange(EXPERTS, dtype=jnp.int32)[None, None, :]).astype(jnp.int32)
    running_count = jnp.cumsum(onehot, axis=1)
    slot_index = jnp.sum(onehot * running_count, axis=2) - 1
    blocks = jnp.arange(N_CTX, dtype=jnp.int32)[:, None]
    targets = flat_ids * rows_all + blocks * CAP + slot_index
    owners = blocks * BIN_CTX + jnp.arange(TOP * BIN_CTX, dtype=jnp.int32)[None, :] // TOP
    row_table = jnp.full((EXPERTS * rows_all,), BINS, jnp.int32).at[targets.reshape(-1)].set(owners.reshape(-1))
    gate_table = jnp.zeros((EXPERTS * rows_all,), jnp.float32).at[targets.reshape(-1)].set(gate_values.reshape(-1).astype(jnp.float32))
    act_pad = jnp.concatenate([activated, jnp.zeros((D, 1), jnp.bfloat16)], axis=1)
    grad_pad = jnp.concatenate([grad_float, jnp.zeros((D, 1), jnp.float32)], axis=1)

    def one_expert(expert):
        chosen = lax.dynamic_slice_in_dim(row_table, expert * rows_all, rows_all)
        weights = lax.dynamic_slice_in_dim(gate_table, expert * rows_all, rows_all)
        rows_in = act_pad[:, chosen]
        rows_grad = (grad_pad[:, chosen] * weights[None, :]).astype(jnp.bfloat16)
        part_in, part_out, part_rows = expert_pass(expert_in[expert], expert_out[expert], rows_in, rows_grad)
        return part_in.astype(jnp.bfloat16), part_out.astype(jnp.bfloat16), part_rows.astype(jnp.bfloat16)

    grad_first, grad_second, grad_back = lax.map(one_expert, jnp.arange(EXPERTS, dtype=jnp.int32))
    back_flat = jnp.transpose(grad_back, (1, 0, 2)).reshape(D, EXPERTS * rows_all).astype(jnp.float32)
    per_bin = targets.reshape(BINS, TOP)
    grad_total = grad_float
    for column in range(TOP):
        grad_total = grad_total + back_flat[:, per_bin[:, column]]
    grad_pre_conv = (grad_total * gelu_slope(pre_float)).astype(jnp.bfloat16)
    margin = KERNEL // 2
    padded_grad = jnp.pad(grad_pre_conv, ((0, 0), (margin, margin)))
    padded_in = jnp.pad(inputs, ((0, 0), (margin, margin)))
    conv_back = jnp.zeros((D, BINS), jnp.float32)
    tap_grads = []
    for offset in range(KERNEL):
        lower = 2 * margin - offset
        conv_back = conv_back + product(conv_weight[offset], padded_grad[:, lower:lower + BINS], ((1,), (0,)))
        tap_grads.append(product(padded_in[:, offset:offset + BINS], grad_pre_conv, ((1,), (1,))))
    grad_inputs = (grad_total + conv_back).astype(jnp.bfloat16)
    return grad_inputs, jnp.stack(tap_grads), grad_first, grad_second
```

```python
import jax
import jax.numpy as jnp
from jax import lax
from jax.sharding import PartitionSpec as P

BF16 = jnp.bfloat16
F32 = jnp.float32


def gelu_value(values):
    factor = 0.7978845608028654
    return 0.5 * values * (1.0 + jnp.tanh(factor * (values + 0.044715 * values * values * values)))


def gelu_slope(values):
    factor = 0.7978845608028654
    tangent = jnp.tanh(factor * (values + 0.044715 * values * values * values))
    return 0.5 * (1.0 + tangent) + 0.5 * values * (1.0 - tangent * tangent) * factor * (
        1.0 + 0.134145 * values * values
    )


def product(left, right, dims):
    return lax.dot_general(left, right, (dims, ((), ())), preferred_element_type=F32)


def swapped(block):
    return lax.ppermute(block, "ctx", [(0, 1), (1, 0)])


def local(inputs, pre_act, grad_out, conv_weight, expert_ids, gate_values, expert_in, expert_out):
    channels, bins = inputs.shape
    experts = lax.axis_size("exp")
    groups = lax.axis_size("ctx")
    capacity = 4 * bins // experts
    width = channels * experts
    kernel = conv_weight.shape[0]
    margin = kernel // 2
    pair = groups == 2
    me = lax.axis_index("ctx")

    ids = expert_ids.T
    names = jnp.arange(experts, dtype=jnp.int32)[:, None]
    chosen = [ids[k][None, :] == names for k in range(ids.shape[0])]
    named = sum(c.astype(BF16) for c in chosen)
    spot = jnp.arange(bins, dtype=jnp.int32)
    earlier = product(named, (spot[:, None] < spot[None, :]).astype(BF16), ((1,), (0,)))
    rows = jnp.arange(experts * capacity, dtype=jnp.int32)[:, None]
    picks = []
    for k, c in enumerate(chosen):
        slot = jnp.sum(jnp.where(c, earlier, 0.0), axis=0).astype(jnp.int32)
        picks.append((rows == (ids[k] * capacity + slot)[None, :]).astype(BF16))
    pick_any = sum(picks)
    pick_each = jnp.concatenate(picks, axis=1)

    pre_float = pre_act.astype(F32)
    grad_float = grad_out.astype(F32)
    activated = (inputs.astype(F32) + gelu_value(pre_float)).astype(BF16)
    gates = gate_values.T
    gated = jnp.concatenate(
        [(grad_float * gates[k][None, :]).astype(BF16) for k in range(len(picks))], axis=1
    )

    def to_experts(cells, pick):
        found = product(cells, pick, ((1,), (1,))).astype(BF16)
        found = found.reshape(channels, experts, capacity).transpose(1, 0, 2)
        found = lax.all_to_all(found, "exp", split_axis=0, concat_axis=0, tiled=True)
        found = found.reshape(width, capacity)
        if pair:
            return jnp.concatenate([found, swapped(found)], axis=1)
        return lax.all_gather(found, "ctx", axis=1, tiled=True)

    rows_in = to_experts(activated, pick_any)
    rows_grad = to_experts(gated, pick_each)

    first = expert_in[0]
    second = expert_out[0]
    hidden = product(first, rows_in, ((0,), (0,)))
    grad_hidden = product(second, rows_grad, ((1,), (0,)))
    grad_pre = (grad_hidden * gelu_slope(hidden)).astype(BF16)
    if pair:
        theirs = product(first, grad_pre[:, capacity:], ((1,), (0,))).astype(BF16)
        mine = product(first, grad_pre[:, :capacity], ((1,), (0,)))
        back = (mine + swapped(theirs).astype(F32)).astype(BF16)
    else:
        part = product(first, grad_pre, ((1,), (0,)))
        back = lax.psum_scatter(part, "ctx", scatter_dimension=1, tiled=True).astype(BF16)
    squashed = gelu_value(hidden).astype(BF16)
    grad_second = product(squashed, rows_grad, ((1,), (1,))).astype(BF16)
    grad_first = product(rows_in, grad_pre, ((1,), (1,))).astype(BF16)

    back = lax.all_to_all(
        back.reshape(experts, channels, capacity), "exp", split_axis=0, concat_axis=0, tiled=True
    )
    back = back.transpose(1, 0, 2).reshape(channels, experts * capacity)
    grad_total = grad_float + product(back, pick_any, ((1,), (0,)))
    grad_pre_conv = (grad_total * gelu_slope(pre_float)).astype(BF16)

    share = experts // groups
    moves = [
        (c * experts + e, (e // share) * experts + c * share + e % share)
        for c in range(groups)
        for e in range(experts)
    ]
    moved = lax.ppermute(grad_pre_conv, ("ctx", "exp"), moves)
    blocks = lax.all_gather(moved, "exp", axis=0, tiled=True).reshape(groups, -1, bins)

    if pair:
        other = swapped(inputs)
        low = jnp.where(me == 0, inputs, other)
        high = jnp.where(me == 0, other, inputs)
        all_inputs = jnp.concatenate([low, high], axis=1)
    else:
        all_inputs = lax.all_gather(inputs, "ctx", axis=1, tiled=True)
    total = groups * bins
    padded = jnp.pad(all_inputs, ((0, 0), (margin, margin)))
    shifted = jnp.concatenate([padded[:, k : k + total] for k in range(kernel)], axis=0)
    weight = conv_weight.reshape(kernel * channels, -1)
    spread = jnp.concatenate(
        [product(weight, blocks[c], ((1,), (0,))) for c in range(groups)], axis=1
    )
    spread = jnp.pad(spread.reshape(kernel, channels, total), ((0, 0), (0, 0), (margin, margin)))
    conv_back = sum(
        spread[k, :, 2 * margin - k : 2 * margin - k + total] for k in range(kernel)
    )
    if pair:
        low, high = conv_back[:, :bins], conv_back[:, bins:]
        mine = jnp.where(me == 0, low, high)
        theirs = jnp.where(me == 0, high, low).astype(BF16)
        conv_back = mine + swapped(theirs).astype(F32)
    else:
        conv_back = lax.psum_scatter(conv_back, "ctx", scatter_dimension=1, tiled=True)
    grad_inputs = (grad_total + conv_back).astype(BF16)
    grad_conv = sum(
        product(shifted[:, c * bins : (c + 1) * bins], blocks[c], ((1,), (1,)))
        for c in range(groups)
    )
    return (
        grad_inputs,
        grad_conv.reshape(kernel, channels, -1),
        grad_first[None],
        grad_second[None],
    )


def solution(mesh):
    placed = (
        P("exp", "ctx"),
        P("exp", "ctx"),
        P("exp", "ctx"),
        P(None, "exp", "ctx"),
        P("ctx", None),
        P("ctx", None),
        P("exp", None, "ctx"),
        P("exp", "ctx", None),
    )
    return jax.shard_map(
        local,
        mesh=mesh,
        in_specs=placed,
        out_specs=(
            P("exp", "ctx"),
            P(None, "exp", "ctx"),
            P("exp", None, "ctx"),
            P("exp", "ctx", None),
        ),
        check_vma=False,
    )
```

```python
import jax
import jax.numpy as jnp
from jax import lax
from jax.experimental import pallas as pl
from jax.experimental.pallas import tpu as pltpu
from jax.sharding import PartitionSpec as P

BF16 = jnp.bfloat16
F32 = jnp.float32


def gelu_value(values):
    factor = 0.7978845608028654
    return 0.5 * values * (1.0 + jnp.tanh(factor * (values + 0.044715 * values * values * values)))


def gelu_slope(values):
    factor = 0.7978845608028654
    tangent = jnp.tanh(factor * (values + 0.044715 * values * values * values))
    return 0.5 * (1.0 + tangent) + 0.5 * values * (1.0 - tangent * tangent) * factor * (
        1.0 + 0.134145 * values * values
    )


def product(left, right, dims):
    return lax.dot_general(left, right, (dims, ((), ())), preferred_element_type=F32)


def swapped(block):
    return lax.ppermute(block, "ctx", [(0, 1), (1, 0)])


def greet(barrier, peers):
    for peer in peers:
        pl.semaphore_signal(barrier, inc=1, device_id=peer, device_id_type=pl.DeviceIdType.MESH)


def remote(source, target, sent, received, device):
    return pltpu.make_async_remote_copy(
        src_ref=source,
        dst_ref=target,
        send_sem=sent,
        recv_sem=received,
        device_id=device,
        device_id_type=pl.DeviceIdType.MESH,
    )


def gather_kernel(cells, out, move_sem, z_sent, z_got, x_sent, x_got, c_sent, c_got):
    c, e = lax.axis_index("ctx"), lax.axis_index("exp")
    size = out.shape[0]
    share = size // 2
    high, low = lax.div(e, share), lax.rem(e, share)
    there = (high, c * share + low)
    across = e + 2 - 4 * lax.rem(lax.div(e, 2), 2)
    twin = e + 1 - 2 * lax.rem(e, 2)
    steps = size // 4
    ring = [lax.rem(e + 4 * d, size) for d in range(1, steps)]
    barrier = pltpu.get_barrier_semaphore()

    @pl.when(high != c)
    def _():
        greet(barrier, [there])

    greet(barrier, [(c, r) for r in ring] + [(c, across), (c, twin)])
    pl.semaphore_wait(barrier, steps + 1 + (high != c).astype(jnp.int32))

    @pl.when(high != c)
    def _():
        remote(cells, out.at[there[1]], move_sem.at[0], move_sem.at[1], there).start()
        remote(cells, out.at[there[1]], move_sem.at[0], move_sem.at[1], there).wait_send()
        remote(cells, out.at[e], move_sem.at[0], move_sem.at[1], there).wait_recv()

    @pl.when(high == c)
    def _():
        copy = pltpu.make_async_copy(cells, out.at[e], move_sem.at[0])
        copy.start()
        copy.wait()

    def back(base, d):
        return lax.rem(base + size - 4 * d, size)

    def along_z(slot, d):
        return remote(
            out.at[slot], out.at[slot], z_sent.at[d - 1], z_got.at[d - 1], (c, ring[d - 1])
        )

    def along_x(slot, j):
        return remote(out.at[slot], out.at[slot], x_sent.at[j], x_got.at[j], (c, across))

    def to_twin(slot, j):
        return remote(out.at[slot], out.at[slot], c_sent.at[j], c_got.at[j], (c, twin))

    for d in range(1, steps):
        along_z(e, d).start()
    along_x(e, 0).start()
    to_twin(e, 0).start()
    for d in range(steps):
        if d:
            along_z(back(e, d), d).wait_recv()
            along_x(back(e, d), d).start()
            to_twin(back(e, d), d).start()
        along_x(back(across, d), d).wait_recv()
        to_twin(back(across, d), steps + d).start()
    twin_across = twin + across - e
    for d in range(steps):
        to_twin(back(twin, d), d).wait_recv()
        to_twin(back(twin_across, d), steps + d).wait_recv()
    for d in range(1, steps):
        along_z(e, d).wait_send()
    for d in range(steps):
        along_x(back(e, d), d).wait_send()
        to_twin(back(e, d), d).wait_send()
        to_twin(back(across, d), steps + d).wait_send()


def gathered(cells, size):
    steps = size // 4
    dma = pltpu.SemaphoreType.DMA
    return pl.pallas_call(
        gather_kernel,
        out_shape=jax.ShapeDtypeStruct((size,) + cells.shape, cells.dtype),
        in_specs=[pl.BlockSpec(memory_space=pltpu.VMEM)],
        out_specs=pl.BlockSpec(memory_space=pltpu.VMEM),
        scratch_shapes=[
            dma((2,)),
            dma((steps - 1,)),
            dma((steps - 1,)),
            dma((steps,)),
            dma((steps,)),
            dma((2 * steps,)),
            dma((2 * steps,)),
        ],
        compiler_params=pltpu.CompilerParams(
            collective_id=0, has_side_effects=True, vmem_limit_bytes=24 * 2**20
        ),
    )(cells)


def local(inputs, pre_act, grad_out, conv_weight, expert_ids, gate_values, expert_in, expert_out):
    channels, bins = inputs.shape
    experts = lax.axis_size("exp")
    groups = lax.axis_size("ctx")
    capacity = 4 * bins // experts
    width = channels * experts
    kernel = conv_weight.shape[0]
    margin = kernel // 2
    pair = groups == 2
    me = lax.axis_index("ctx")

    ids = expert_ids.T
    names = jnp.arange(experts, dtype=jnp.int32)[:, None]
    chosen = [ids[k][None, :] == names for k in range(ids.shape[0])]
    named = sum(c.astype(BF16) for c in chosen)
    spot = jnp.arange(bins, dtype=jnp.int32)
    earlier = product(named, (spot[:, None] < spot[None, :]).astype(BF16), ((1,), (0,)))
    rows = jnp.arange(experts * capacity, dtype=jnp.int32)[:, None]
    picks = []
    for k, c in enumerate(chosen):
        slot = jnp.sum(jnp.where(c, earlier, 0.0), axis=0).astype(jnp.int32)
        picks.append((rows == (ids[k] * capacity + slot)[None, :]).astype(BF16))
    pick_any = sum(picks)
    pick_each = jnp.concatenate(picks, axis=1)

    pre_float = pre_act.astype(F32)
    grad_float = grad_out.astype(F32)
    activated = (inputs.astype(F32) + gelu_value(pre_float)).astype(BF16)
    gates = gate_values.T
    gated = jnp.concatenate(
        [(grad_float * gates[k][None, :]).astype(BF16) for k in range(len(picks))], axis=1
    )

    def to_experts(cells, pick):
        found = product(cells, pick, ((1,), (1,))).astype(BF16)
        found = found.reshape(channels, experts, capacity).transpose(1, 0, 2)
        found = lax.all_to_all(found, "exp", split_axis=0, concat_axis=0, tiled=True)
        found = found.reshape(width, capacity)
        if pair:
            return jnp.concatenate([found, swapped(found)], axis=1)
        return lax.all_gather(found, "ctx", axis=1, tiled=True)

    rows_in = to_experts(activated, pick_any)
    rows_grad = to_experts(gated, pick_each)

    first = expert_in[0]
    second = expert_out[0]
    hidden = product(first, rows_in, ((0,), (0,)))
    grad_hidden = product(second, rows_grad, ((1,), (0,)))
    grad_pre = (grad_hidden * gelu_slope(hidden)).astype(BF16)
    if pair:
        theirs = product(first, grad_pre[:, capacity:], ((1,), (0,))).astype(BF16)
        mine = product(first, grad_pre[:, :capacity], ((1,), (0,)))
        back = (mine + swapped(theirs).astype(F32)).astype(BF16)
    else:
        part = product(first, grad_pre, ((1,), (0,)))
        back = lax.psum_scatter(part, "ctx", scatter_dimension=1, tiled=True).astype(BF16)
    squashed = gelu_value(hidden).astype(BF16)
    grad_second = product(squashed, rows_grad, ((1,), (1,))).astype(BF16)
    grad_first = product(rows_in, grad_pre, ((1,), (1,))).astype(BF16)

    back = lax.all_to_all(
        back.reshape(experts, channels, capacity), "exp", split_axis=0, concat_axis=0, tiled=True
    )
    back = back.transpose(1, 0, 2).reshape(channels, experts * capacity)
    grad_total = grad_float + product(back, pick_any, ((1,), (0,)))
    grad_pre_conv = (grad_total * gelu_slope(pre_float)).astype(BF16)

    share = experts // groups
    if pair and experts == 16:
        blocks = gathered(grad_pre_conv, experts).reshape(groups, -1, bins)
    else:
        moves = [
            (c * experts + e, (e // share) * experts + c * share + e % share)
            for c in range(groups)
            for e in range(experts)
        ]
        moved = lax.ppermute(grad_pre_conv, ("ctx", "exp"), moves)
        blocks = lax.all_gather(moved, "exp", axis=0, tiled=True).reshape(groups, -1, bins)

    if pair:
        other = swapped(inputs)
        low = jnp.where(me == 0, inputs, other)
        high = jnp.where(me == 0, other, inputs)
        all_inputs = jnp.concatenate([low, high], axis=1)
    else:
        all_inputs = lax.all_gather(inputs, "ctx", axis=1, tiled=True)
    total = groups * bins
    padded = jnp.pad(all_inputs, ((0, 0), (margin, margin)))
    shifted = jnp.concatenate([padded[:, k : k + total] for k in range(kernel)], axis=0)
    weight = conv_weight.reshape(kernel * channels, -1)
    spread = jnp.concatenate(
        [product(weight, blocks[c], ((1,), (0,))) for c in range(groups)], axis=1
    )
    spread = jnp.pad(spread.reshape(kernel, channels, total), ((0, 0), (0, 0), (margin, margin)))
    conv_back = sum(
        spread[k, :, 2 * margin - k : 2 * margin - k + total] for k in range(kernel)
    )
    if pair:
        low, high = conv_back[:, :bins], conv_back[:, bins:]
        mine = jnp.where(me == 0, low, high)
        theirs = jnp.where(me == 0, high, low).astype(BF16)
        conv_back = mine + swapped(theirs).astype(F32)
    else:
        conv_back = lax.psum_scatter(conv_back, "ctx", scatter_dimension=1, tiled=True)
    grad_inputs = (grad_total + conv_back).astype(BF16)
    grad_conv = sum(
        product(shifted[:, c * bins : (c + 1) * bins], blocks[c], ((1,), (1,)))
        for c in range(groups)
    )
    return (
        grad_inputs,
        grad_conv.reshape(kernel, channels, -1),
        grad_first[None],
        grad_second[None],
    )


def solution(mesh):
    placed = (
        P("exp", "ctx"),
        P("exp", "ctx"),
        P("exp", "ctx"),
        P(None, "exp", "ctx"),
        P("ctx", None),
        P("ctx", None),
        P("exp", None, "ctx"),
        P("exp", "ctx", None),
    )
    return jax.shard_map(
        local,
        mesh=mesh,
        in_specs=placed,
        out_specs=(
            P("exp", "ctx"),
            P(None, "exp", "ctx"),
            P("exp", None, "ctx"),
            P("exp", "ctx", None),
        ),
        check_vma=False,
    )
```

```python
import jax
import jax.numpy as jnp
from jax import lax
from jax.experimental import pallas as pl
from jax.experimental.pallas import tpu as pltpu
from jax.sharding import PartitionSpec as P

BF16 = jnp.bfloat16
F32 = jnp.float32


def gelu_value(values):
    factor = 0.7978845608028654
    return 0.5 * values * (1.0 + jnp.tanh(factor * (values + 0.044715 * values * values * values)))


def gelu_slope(values):
    factor = 0.7978845608028654
    tangent = jnp.tanh(factor * (values + 0.044715 * values * values * values))
    return 0.5 * (1.0 + tangent) + 0.5 * values * (1.0 - tangent * tangent) * factor * (
        1.0 + 0.134145 * values * values
    )


def product(left, right, dims):
    return lax.dot_general(left, right, (dims, ((), ())), preferred_element_type=F32)


def swapped(block):
    return lax.ppermute(block, "ctx", [(0, 1), (1, 0)])


def greet(barrier, peers):
    for peer in peers:
        pl.semaphore_signal(barrier, inc=1, device_id=peer, device_id_type=pl.DeviceIdType.MESH)


def remote(source, target, sent, received, device):
    return pltpu.make_async_remote_copy(
        src_ref=source,
        dst_ref=target,
        send_sem=sent,
        recv_sem=received,
        device_id=device,
        device_id_type=pl.DeviceIdType.MESH,
    )


def gather_kernel(cells, out, move_sem, z_sent, z_got, x_sent, x_got, c_sent, c_got):
    c, e = lax.axis_index("ctx"), lax.axis_index("exp")
    size = out.shape[0]
    share = size // 2
    high, low = lax.div(e, share), lax.rem(e, share)
    there = (high, c * share + low)
    across = e + 2 - 4 * lax.rem(lax.div(e, 2), 2)
    twin = e + 1 - 2 * lax.rem(e, 2)
    steps = size // 4
    ring = [lax.rem(e + 4 * d, size) for d in range(1, steps)]
    barrier = pltpu.get_barrier_semaphore()

    @pl.when(high != c)
    def _():
        greet(barrier, [there])

    greet(barrier, [(c, r) for r in ring] + [(c, across), (c, twin)])
    pl.semaphore_wait(barrier, steps + 1 + (high != c).astype(jnp.int32))

    @pl.when(high != c)
    def _():
        remote(cells, out.at[there[1]], move_sem.at[0], move_sem.at[1], there).start()
        remote(cells, out.at[there[1]], move_sem.at[0], move_sem.at[1], there).wait_send()
        remote(cells, out.at[e], move_sem.at[0], move_sem.at[1], there).wait_recv()

    @pl.when(high == c)
    def _():
        copy = pltpu.make_async_copy(cells, out.at[e], move_sem.at[0])
        copy.start()
        copy.wait()

    def back(base, d):
        return lax.rem(base + size - 4 * d, size)

    def along_z(slot, d):
        return remote(
            out.at[slot], out.at[slot], z_sent.at[d - 1], z_got.at[d - 1], (c, ring[d - 1])
        )

    def along_x(slot, j):
        return remote(out.at[slot], out.at[slot], x_sent.at[j], x_got.at[j], (c, across))

    def to_twin(slot, j):
        return remote(out.at[slot], out.at[slot], c_sent.at[j], c_got.at[j], (c, twin))

    for d in range(1, steps):
        along_z(e, d).start()
    along_x(e, 0).start()
    to_twin(e, 0).start()
    for d in range(steps):
        if d:
            along_z(back(e, d), d).wait_recv()
            along_x(back(e, d), d).start()
            to_twin(back(e, d), d).start()
        along_x(back(across, d), d).wait_recv()
        to_twin(back(across, d), steps + d).start()
    twin_across = twin + across - e
    for d in range(steps):
        to_twin(back(twin, d), d).wait_recv()
        to_twin(back(twin_across, d), steps + d).wait_recv()
    for d in range(1, steps):
        along_z(e, d).wait_send()
    for d in range(steps):
        along_x(back(e, d), d).wait_send()
        to_twin(back(e, d), d).wait_send()
        to_twin(back(across, d), steps + d).wait_send()


def gathered(cells, size):
    steps = size // 4
    dma = pltpu.SemaphoreType.DMA
    return pl.pallas_call(
        gather_kernel,
        out_shape=jax.ShapeDtypeStruct((size,) + cells.shape, cells.dtype),
        in_specs=[pl.BlockSpec(memory_space=pltpu.VMEM)],
        out_specs=pl.BlockSpec(memory_space=pltpu.VMEM),
        scratch_shapes=[
            dma((2,)),
            dma((steps - 1,)),
            dma((steps - 1,)),
            dma((steps,)),
            dma((steps,)),
            dma((2 * steps,)),
            dma((2 * steps,)),
        ],
        compiler_params=pltpu.CompilerParams(
            collective_id=0, has_side_effects=True, vmem_limit_bytes=24 * 2**20
        ),
    )(cells)


def spread_kernel(cells, out, a_sent, a_got, y_sent, y_got):
    c, e = lax.axis_index("ctx"), lax.axis_index("exp")
    size = cells.shape[0]
    other = (1 - c, e)

    def to(d):
        return lax.rem(e + d, size)

    def source(d):
        return lax.rem(e + size - d, size)

    barrier = pltpu.get_barrier_semaphore()
    greet(barrier, [(c, to(d)) for d in range(1, size)] + [other])
    pl.semaphore_wait(barrier, size)

    def sending(d):
        return remote(cells.at[to(d)], out.at[0, e], a_sent.at[d], a_got.at[d], (c, to(d)))

    def arriving(d):
        slot = source(d)
        return remote(cells.at[slot], out.at[0, slot], a_sent.at[d], a_got.at[d], (c, slot))

    def handing(d):
        slot = source(d)
        return remote(out.at[0, slot], out.at[1, slot], y_sent.at[d], y_got.at[d], other)

    mine = remote(cells.at[e], out.at[1, e], y_sent.at[0], y_got.at[0], other)
    mine.start()
    for d in range(1, size):
        sending(d).start()
    kept = pltpu.make_async_copy(cells.at[e], out.at[0, e], a_sent.at[0])
    kept.start()
    for d in range(1, size):
        arriving(d).wait_recv()
        handing(d).start()
    kept.wait()
    mine.wait()
    for d in range(1, size):
        handing(d).wait()
        sending(d).wait_send()


def spread_rows(cells):
    size = cells.shape[0]
    dma = pltpu.SemaphoreType.DMA
    return pl.pallas_call(
        spread_kernel,
        out_shape=jax.ShapeDtypeStruct((2,) + cells.shape, cells.dtype),
        in_specs=[pl.BlockSpec(memory_space=pltpu.VMEM)],
        out_specs=pl.BlockSpec(memory_space=pltpu.VMEM),
        scratch_shapes=[dma((size,)), dma((size,)), dma((size,)), dma((size,))],
        compiler_params=pltpu.CompilerParams(
            collective_id=1, has_side_effects=True, vmem_limit_bytes=24 * 2**20
        ),
    )(cells)


def local(inputs, pre_act, grad_out, conv_weight, expert_ids, gate_values, expert_in, expert_out):
    channels, bins = inputs.shape
    experts = lax.axis_size("exp")
    groups = lax.axis_size("ctx")
    capacity = 4 * bins // experts
    width = channels * experts
    kernel = conv_weight.shape[0]
    margin = kernel // 2
    pair = groups == 2
    me = lax.axis_index("ctx")

    ids = expert_ids.T
    names = jnp.arange(experts, dtype=jnp.int32)[:, None]
    chosen = [ids[k][None, :] == names for k in range(ids.shape[0])]
    named = sum(c.astype(BF16) for c in chosen)
    spot = jnp.arange(bins, dtype=jnp.int32)
    earlier = product(named, (spot[:, None] < spot[None, :]).astype(BF16), ((1,), (0,)))
    rows = jnp.arange(experts * capacity, dtype=jnp.int32)[:, None]
    picks = []
    for k, c in enumerate(chosen):
        slot = jnp.sum(jnp.where(c, earlier, 0.0), axis=0).astype(jnp.int32)
        picks.append((rows == (ids[k] * capacity + slot)[None, :]).astype(BF16))
    pick_any = sum(picks)
    pick_each = jnp.concatenate(picks, axis=1)

    pre_float = pre_act.astype(F32)
    grad_float = grad_out.astype(F32)
    activated = (inputs.astype(F32) + gelu_value(pre_float)).astype(BF16)
    gates = gate_values.T
    gated = jnp.concatenate(
        [(grad_float * gates[k][None, :]).astype(BF16) for k in range(len(picks))], axis=1
    )

    def picked(cells, pick):
        found = product(cells, pick, ((1,), (1,))).astype(BF16)
        return found.reshape(channels, experts, capacity).transpose(1, 0, 2)

    def to_experts(found):
        found = lax.all_to_all(found, "exp", split_axis=0, concat_axis=0, tiled=True)
        found = found.reshape(width, capacity)
        if pair:
            return jnp.concatenate([found, swapped(found)], axis=1)
        return lax.all_gather(found, "ctx", axis=1, tiled=True)

    sent_in = picked(activated, pick_any)
    sent_grad = picked(gated, pick_each)
    if pair and experts == 16:
        both = spread_rows(jnp.concatenate([sent_in, sent_grad], axis=1))
        rows_in, rows_grad = [
            jnp.concatenate([half[0].reshape(width, -1), half[1].reshape(width, -1)], axis=1)
            for half in (both[:, :, :channels], both[:, :, channels:])
        ]
    else:
        rows_in = to_experts(sent_in)
        rows_grad = to_experts(sent_grad)

    first = expert_in[0]
    second = expert_out[0]
    hidden = product(first, rows_in, ((0,), (0,)))
    grad_hidden = product(second, rows_grad, ((1,), (0,)))
    grad_pre = (grad_hidden * gelu_slope(hidden)).astype(BF16)
    if pair:
        theirs = product(first, grad_pre[:, capacity:], ((1,), (0,))).astype(BF16)
        mine = product(first, grad_pre[:, :capacity], ((1,), (0,)))
        back = (mine + swapped(theirs).astype(F32)).astype(BF16)
    else:
        part = product(first, grad_pre, ((1,), (0,)))
        back = lax.psum_scatter(part, "ctx", scatter_dimension=1, tiled=True).astype(BF16)
    squashed = gelu_value(hidden).astype(BF16)
    grad_second = product(squashed, rows_grad, ((1,), (1,))).astype(BF16)
    grad_first = product(rows_in, grad_pre, ((1,), (1,))).astype(BF16)

    back = lax.all_to_all(
        back.reshape(experts, channels, capacity), "exp", split_axis=0, concat_axis=0, tiled=True
    )
    back = back.transpose(1, 0, 2).reshape(channels, experts * capacity)
    grad_total = grad_float + product(back, pick_any, ((1,), (0,)))
    grad_pre_conv = (grad_total * gelu_slope(pre_float)).astype(BF16)

    share = experts // groups
    if pair and experts == 16:
        blocks = gathered(grad_pre_conv, experts).reshape(groups, -1, bins)
    else:
        moves = [
            (c * experts + e, (e // share) * experts + c * share + e % share)
            for c in range(groups)
            for e in range(experts)
        ]
        moved = lax.ppermute(grad_pre_conv, ("ctx", "exp"), moves)
        blocks = lax.all_gather(moved, "exp", axis=0, tiled=True).reshape(groups, -1, bins)

    if pair:
        other = swapped(inputs)
        low = jnp.where(me == 0, inputs, other)
        high = jnp.where(me == 0, other, inputs)
        all_inputs = jnp.concatenate([low, high], axis=1)
    else:
        all_inputs = lax.all_gather(inputs, "ctx", axis=1, tiled=True)
    total = groups * bins
    padded = jnp.pad(all_inputs, ((0, 0), (margin, margin)))
    shifted = jnp.concatenate([padded[:, k : k + total] for k in range(kernel)], axis=0)
    weight = conv_weight.reshape(kernel * channels, -1)
    spread = jnp.concatenate(
        [product(weight, blocks[c], ((1,), (0,))) for c in range(groups)], axis=1
    )
    spread = jnp.pad(spread.reshape(kernel, channels, total), ((0, 0), (0, 0), (margin, margin)))
    conv_back = sum(
        spread[k, :, 2 * margin - k : 2 * margin - k + total] for k in range(kernel)
    )
    if pair:
        low, high = conv_back[:, :bins], conv_back[:, bins:]
        mine = jnp.where(me == 0, low, high)
        theirs = jnp.where(me == 0, high, low).astype(BF16)
        conv_back = mine + swapped(theirs).astype(F32)
    else:
        conv_back = lax.psum_scatter(conv_back, "ctx", scatter_dimension=1, tiled=True)
    grad_inputs = (grad_total + conv_back).astype(BF16)
    grad_conv = sum(
        product(shifted[:, c * bins : (c + 1) * bins], blocks[c], ((1,), (1,)))
        for c in range(groups)
    )
    return (
        grad_inputs,
        grad_conv.reshape(kernel, channels, -1),
        grad_first[None],
        grad_second[None],
    )


def solution(mesh):
    placed = (
        P("exp", "ctx"),
        P("exp", "ctx"),
        P("exp", "ctx"),
        P(None, "exp", "ctx"),
        P("ctx", None),
        P("ctx", None),
        P("exp", None, "ctx"),
        P("exp", "ctx", None),
    )
    return jax.shard_map(
        local,
        mesh=mesh,
        in_specs=placed,
        out_specs=(
            P("exp", "ctx"),
            P(None, "exp", "ctx"),
            P("exp", None, "ctx"),
            P("exp", "ctx", None),
        ),
        check_vma=False,
    )
```

```python
import jax
import jax.numpy as jnp
from jax import lax
from jax.experimental import pallas as pl
from jax.experimental.pallas import tpu as pltpu
from jax.sharding import PartitionSpec as P

BF16 = jnp.bfloat16
F32 = jnp.float32


def gelu_value(values):
    factor = 0.7978845608028654
    return 0.5 * values * (1.0 + jnp.tanh(factor * (values + 0.044715 * values * values * values)))


def gelu_slope(values):
    factor = 0.7978845608028654
    tangent = jnp.tanh(factor * (values + 0.044715 * values * values * values))
    return 0.5 * (1.0 + tangent) + 0.5 * values * (1.0 - tangent * tangent) * factor * (
        1.0 + 0.134145 * values * values
    )


def product(left, right, dims):
    return lax.dot_general(left, right, (dims, ((), ())), preferred_element_type=F32)


def swapped(block):
    return lax.ppermute(block, "ctx", [(0, 1), (1, 0)])


def greet(barrier, peers):
    for peer in peers:
        pl.semaphore_signal(barrier, inc=1, device_id=peer, device_id_type=pl.DeviceIdType.MESH)


def remote(source, target, sent, received, device):
    return pltpu.make_async_remote_copy(
        src_ref=source,
        dst_ref=target,
        send_sem=sent,
        recv_sem=received,
        device_id=device,
        device_id_type=pl.DeviceIdType.MESH,
    )


def gather_kernel(cells, out, move_sem, z_sent, z_got, x_sent, x_got, c_sent, c_got):
    c, e = lax.axis_index("ctx"), lax.axis_index("exp")
    size = out.shape[0]
    share = size // 2
    high, low = lax.div(e, share), lax.rem(e, share)
    there = (high, c * share + low)
    across = e + 2 - 4 * lax.rem(lax.div(e, 2), 2)
    twin = e + 1 - 2 * lax.rem(e, 2)
    steps = size // 4
    ring = [lax.rem(e + 4 * d, size) for d in range(1, steps)]
    barrier = pltpu.get_barrier_semaphore()

    @pl.when(high != c)
    def _():
        greet(barrier, [there])

    greet(barrier, [(c, r) for r in ring] + [(c, across), (c, twin)])
    pl.semaphore_wait(barrier, steps + 1 + (high != c).astype(jnp.int32))

    @pl.when(high != c)
    def _():
        remote(cells, out.at[there[1]], move_sem.at[0], move_sem.at[1], there).start()
        remote(cells, out.at[there[1]], move_sem.at[0], move_sem.at[1], there).wait_send()
        remote(cells, out.at[e], move_sem.at[0], move_sem.at[1], there).wait_recv()

    @pl.when(high == c)
    def _():
        copy = pltpu.make_async_copy(cells, out.at[e], move_sem.at[0])
        copy.start()
        copy.wait()

    def back(base, d):
        return lax.rem(base + size - 4 * d, size)

    def along_z(slot, d):
        return remote(
            out.at[slot], out.at[slot], z_sent.at[d - 1], z_got.at[d - 1], (c, ring[d - 1])
        )

    def along_x(slot, j):
        return remote(out.at[slot], out.at[slot], x_sent.at[j], x_got.at[j], (c, across))

    def to_twin(slot, j):
        return remote(out.at[slot], out.at[slot], c_sent.at[j], c_got.at[j], (c, twin))

    for d in range(1, steps):
        along_z(e, d).start()
    along_x(e, 0).start()
    to_twin(e, 0).start()
    for d in range(steps):
        if d:
            along_z(back(e, d), d).wait_recv()
            along_x(back(e, d), d).start()
            to_twin(back(e, d), d).start()
        along_x(back(across, d), d).wait_recv()
        to_twin(back(across, d), steps + d).start()
    twin_across = twin + across - e
    for d in range(steps):
        to_twin(back(twin, d), d).wait_recv()
        to_twin(back(twin_across, d), steps + d).wait_recv()
    for d in range(1, steps):
        along_z(e, d).wait_send()
    for d in range(steps):
        along_x(back(e, d), d).wait_send()
        to_twin(back(e, d), d).wait_send()
        to_twin(back(across, d), steps + d).wait_send()


def gathered(cells, size):
    steps = size // 4
    dma = pltpu.SemaphoreType.DMA
    return pl.pallas_call(
        gather_kernel,
        out_shape=jax.ShapeDtypeStruct((size,) + cells.shape, cells.dtype),
        in_specs=[pl.BlockSpec(memory_space=pltpu.VMEM)],
        out_specs=pl.BlockSpec(memory_space=pltpu.VMEM),
        scratch_shapes=[
            dma((2,)),
            dma((steps - 1,)),
            dma((steps - 1,)),
            dma((steps,)),
            dma((steps,)),
            dma((2 * steps,)),
            dma((2 * steps,)),
        ],
        compiler_params=pltpu.CompilerParams(
            collective_id=0, has_side_effects=True, vmem_limit_bytes=24 * 2**20
        ),
    )(cells)


def spread_kernel(cells, out, a_sent, a_got, y_sent, y_got):
    c, e = lax.axis_index("ctx"), lax.axis_index("exp")
    size = cells.shape[0]
    other = (1 - c, e)

    def to(d):
        return lax.rem(e + d, size)

    def source(d):
        return lax.rem(e + size - d, size)

    barrier = pltpu.get_barrier_semaphore()
    greet(barrier, [(c, to(d)) for d in range(1, size)] + [other])
    pl.semaphore_wait(barrier, size)

    def sending(d):
        return remote(cells.at[to(d)], out.at[0, e], a_sent.at[d], a_got.at[d], (c, to(d)))

    def arriving(d):
        slot = source(d)
        return remote(cells.at[slot], out.at[0, slot], a_sent.at[d], a_got.at[d], (c, slot))

    def handing(d):
        slot = source(d)
        return remote(out.at[0, slot], out.at[1, slot], y_sent.at[d], y_got.at[d], other)

    mine = remote(cells.at[e], out.at[1, e], y_sent.at[0], y_got.at[0], other)
    mine.start()
    for d in range(1, size):
        sending(d).start()
    kept = pltpu.make_async_copy(cells.at[e], out.at[0, e], a_sent.at[0])
    kept.start()
    for d in range(1, size):
        arriving(d).wait_recv()
        handing(d).start()
    kept.wait()
    mine.wait()
    for d in range(1, size):
        handing(d).wait()
        sending(d).wait_send()


def spread_rows(cells):
    size = cells.shape[0]
    dma = pltpu.SemaphoreType.DMA
    return pl.pallas_call(
        spread_kernel,
        out_shape=jax.ShapeDtypeStruct((2,) + cells.shape, cells.dtype),
        in_specs=[pl.BlockSpec(memory_space=pltpu.VMEM)],
        out_specs=pl.BlockSpec(memory_space=pltpu.VMEM),
        scratch_shapes=[dma((size,)), dma((size,)), dma((size,)), dma((size,))],
        compiler_params=pltpu.CompilerParams(
            collective_id=1, has_side_effects=True, vmem_limit_bytes=24 * 2**20
        ),
    )(cells)


def return_kernel(theirs, mine, out, got, summed, y_sent, y_got, a_sent, a_got):
    c, e = lax.axis_index("ctx"), lax.axis_index("exp")
    size = mine.shape[0]
    other = (1 - c, e)

    def to(d):
        return lax.rem(e + d, size)

    def source(d):
        return lax.rem(e + size - d, size)

    barrier = pltpu.get_barrier_semaphore()
    greet(barrier, [(c, to(d)) for d in range(1, size)] + [other])
    pl.semaphore_wait(barrier, size)

    def crossing(d):
        return remote(theirs.at[to(d)], got.at[to(d)], y_sent.at[d], y_got.at[d], other)

    def sending(d):
        return remote(summed.at[to(d)], out.at[e], a_sent.at[d], a_got.at[d], (c, to(d)))

    def arriving(d):
        slot = source(d)
        return remote(summed.at[slot], out.at[slot], a_sent.at[d], a_got.at[d], (c, slot))

    order = [*range(1, size), 0]
    for d in order:
        crossing(d).start()
    for d in order:
        crossing(d).wait_recv()
        total = (mine[to(d)] + got[to(d)].astype(F32)).astype(BF16)
        if d:
            summed[to(d)] = total
            sending(d).start()
        else:
            out[e] = total
    for d in range(1, size):
        arriving(d).wait_recv()
        sending(d).wait_send()
    for d in order:
        crossing(d).wait_send()


def returned(theirs, mine):
    size = mine.shape[0]
    dma = pltpu.SemaphoreType.DMA
    return pl.pallas_call(
        return_kernel,
        out_shape=jax.ShapeDtypeStruct(theirs.shape, theirs.dtype),
        in_specs=[pl.BlockSpec(memory_space=pltpu.VMEM)] * 2,
        out_specs=pl.BlockSpec(memory_space=pltpu.VMEM),
        scratch_shapes=[pltpu.VMEM(theirs.shape, theirs.dtype)] * 2
        + [dma((size,)), dma((size,)), dma((size,)), dma((size,))],
        compiler_params=pltpu.CompilerParams(
            collective_id=2, has_side_effects=True, vmem_limit_bytes=24 * 2**20
        ),
    )(theirs, mine)


def local(inputs, pre_act, grad_out, conv_weight, expert_ids, gate_values, expert_in, expert_out):
    channels, bins = inputs.shape
    experts = lax.axis_size("exp")
    groups = lax.axis_size("ctx")
    capacity = 4 * bins // experts
    width = channels * experts
    kernel = conv_weight.shape[0]
    margin = kernel // 2
    pair = groups == 2
    me = lax.axis_index("ctx")

    ids = expert_ids.T
    names = jnp.arange(experts, dtype=jnp.int32)[:, None]
    chosen = [ids[k][None, :] == names for k in range(ids.shape[0])]
    named = sum(c.astype(BF16) for c in chosen)
    spot = jnp.arange(bins, dtype=jnp.int32)
    earlier = product(named, (spot[:, None] < spot[None, :]).astype(BF16), ((1,), (0,)))
    rows = jnp.arange(experts * capacity, dtype=jnp.int32)[:, None]
    picks = []
    for k, c in enumerate(chosen):
        slot = jnp.sum(jnp.where(c, earlier, 0.0), axis=0).astype(jnp.int32)
        picks.append((rows == (ids[k] * capacity + slot)[None, :]).astype(BF16))
    pick_any = sum(picks)
    pick_each = jnp.concatenate(picks, axis=1)

    pre_float = pre_act.astype(F32)
    grad_float = grad_out.astype(F32)
    activated = (inputs.astype(F32) + gelu_value(pre_float)).astype(BF16)
    gates = gate_values.T
    gated = jnp.concatenate(
        [(grad_float * gates[k][None, :]).astype(BF16) for k in range(len(picks))], axis=1
    )

    def picked(cells, pick):
        found = product(cells, pick, ((1,), (1,))).astype(BF16)
        return found.reshape(channels, experts, capacity).transpose(1, 0, 2)

    def to_experts(found):
        found = lax.all_to_all(found, "exp", split_axis=0, concat_axis=0, tiled=True)
        found = found.reshape(width, capacity)
        if pair:
            return jnp.concatenate([found, swapped(found)], axis=1)
        return lax.all_gather(found, "ctx", axis=1, tiled=True)

    sent_in = picked(activated, pick_any)
    sent_grad = picked(gated, pick_each)
    if pair and experts == 16:
        both = spread_rows(jnp.concatenate([sent_in, sent_grad], axis=1))
        rows_in, rows_grad = [
            jnp.concatenate([half[0].reshape(width, -1), half[1].reshape(width, -1)], axis=1)
            for half in (both[:, :, :channels], both[:, :, channels:])
        ]
    else:
        rows_in = to_experts(sent_in)
        rows_grad = to_experts(sent_grad)

    first = expert_in[0]
    second = expert_out[0]
    hidden = product(first, rows_in, ((0,), (0,)))
    grad_hidden = product(second, rows_grad, ((1,), (0,)))
    grad_pre = (grad_hidden * gelu_slope(hidden)).astype(BF16)
    if pair:
        theirs = product(first, grad_pre[:, capacity:], ((1,), (0,))).astype(BF16)
        mine = product(first, grad_pre[:, :capacity], ((1,), (0,)))
        if experts != 16:
            back = (mine + swapped(theirs).astype(F32)).astype(BF16)
    else:
        part = product(first, grad_pre, ((1,), (0,)))
        back = lax.psum_scatter(part, "ctx", scatter_dimension=1, tiled=True).astype(BF16)
    squashed = gelu_value(hidden).astype(BF16)
    grad_second = product(squashed, rows_grad, ((1,), (1,))).astype(BF16)
    grad_first = product(rows_in, grad_pre, ((1,), (1,))).astype(BF16)

    shape = (experts, channels, capacity)
    if pair and experts == 16:
        back = returned(theirs.reshape(shape), mine.reshape(shape))
    else:
        back = lax.all_to_all(
            back.reshape(shape), "exp", split_axis=0, concat_axis=0, tiled=True
        )
    back = back.transpose(1, 0, 2).reshape(channels, experts * capacity)
    grad_total = grad_float + product(back, pick_any, ((1,), (0,)))
    grad_pre_conv = (grad_total * gelu_slope(pre_float)).astype(BF16)

    share = experts // groups
    if pair and experts == 16:
        blocks = gathered(grad_pre_conv, experts).reshape(groups, -1, bins)
    else:
        moves = [
            (c * experts + e, (e // share) * experts + c * share + e % share)
            for c in range(groups)
            for e in range(experts)
        ]
        moved = lax.ppermute(grad_pre_conv, ("ctx", "exp"), moves)
        blocks = lax.all_gather(moved, "exp", axis=0, tiled=True).reshape(groups, -1, bins)

    if pair:
        other = swapped(inputs)
        low = jnp.where(me == 0, inputs, other)
        high = jnp.where(me == 0, other, inputs)
        all_inputs = jnp.concatenate([low, high], axis=1)
    else:
        all_inputs = lax.all_gather(inputs, "ctx", axis=1, tiled=True)
    total = groups * bins
    padded = jnp.pad(all_inputs, ((0, 0), (margin, margin)))
    shifted = jnp.concatenate([padded[:, k : k + total] for k in range(kernel)], axis=0)
    weight = conv_weight.reshape(kernel * channels, -1)
    spread = jnp.concatenate(
        [product(weight, blocks[c], ((1,), (0,))) for c in range(groups)], axis=1
    )
    spread = jnp.pad(spread.reshape(kernel, channels, total), ((0, 0), (0, 0), (margin, margin)))
    conv_back = sum(
        spread[k, :, 2 * margin - k : 2 * margin - k + total] for k in range(kernel)
    )
    if pair:
        low, high = conv_back[:, :bins], conv_back[:, bins:]
        mine = jnp.where(me == 0, low, high)
        theirs = jnp.where(me == 0, high, low).astype(BF16)
        conv_back = mine + swapped(theirs).astype(F32)
    else:
        conv_back = lax.psum_scatter(conv_back, "ctx", scatter_dimension=1, tiled=True)
    grad_inputs = (grad_total + conv_back).astype(BF16)
    grad_conv = sum(
        product(shifted[:, c * bins : (c + 1) * bins], blocks[c], ((1,), (1,)))
        for c in range(groups)
    )
    return (
        grad_inputs,
        grad_conv.reshape(kernel, channels, -1),
        grad_first[None],
        grad_second[None],
    )


def solution(mesh):
    placed = (
        P("exp", "ctx"),
        P("exp", "ctx"),
        P("exp", "ctx"),
        P(None, "exp", "ctx"),
        P("ctx", None),
        P("ctx", None),
        P("exp", None, "ctx"),
        P("exp", "ctx", None),
    )
    return jax.shard_map(
        local,
        mesh=mesh,
        in_specs=placed,
        out_specs=(
            P("exp", "ctx"),
            P(None, "exp", "ctx"),
            P("exp", None, "ctx"),
            P("exp", "ctx", None),
        ),
        check_vma=False,
    )
```

```python
import jax
import jax.numpy as jnp
from jax import lax
from jax.experimental import pallas as pl
from jax.experimental.pallas import tpu as pltpu
from jax.sharding import PartitionSpec as P

BF16 = jnp.bfloat16
F32 = jnp.float32


def gelu_value(values):
    factor = 0.7978845608028654
    return 0.5 * values * (1.0 + jnp.tanh(factor * (values + 0.044715 * values * values * values)))


def gelu_slope(values):
    factor = 0.7978845608028654
    tangent = jnp.tanh(factor * (values + 0.044715 * values * values * values))
    return 0.5 * (1.0 + tangent) + 0.5 * values * (1.0 - tangent * tangent) * factor * (
        1.0 + 0.134145 * values * values
    )


def product(left, right, dims):
    return lax.dot_general(left, right, (dims, ((), ())), preferred_element_type=F32)


def swapped(block):
    return lax.ppermute(block, "ctx", [(0, 1), (1, 0)])


def greet(barrier, peers):
    for peer in peers:
        pl.semaphore_signal(barrier, inc=1, device_id=peer, device_id_type=pl.DeviceIdType.MESH)


def remote(source, target, sent, received, device):
    return pltpu.make_async_remote_copy(
        src_ref=source,
        dst_ref=target,
        send_sem=sent,
        recv_sem=received,
        device_id=device,
        device_id_type=pl.DeviceIdType.MESH,
    )


def gather_kernel(cells, out, move_sem, z_sent, z_got, x_sent, x_got, c_sent, c_got):
    c, e = lax.axis_index("ctx"), lax.axis_index("exp")
    size = out.shape[0]
    share = size // 2
    high, low = lax.div(e, share), lax.rem(e, share)
    there = (high, c * share + low)
    across = e + 2 - 4 * lax.rem(lax.div(e, 2), 2)
    twin = e + 1 - 2 * lax.rem(e, 2)
    steps = size // 4
    ring = [lax.rem(e + 4 * d, size) for d in range(1, steps)]
    barrier = pltpu.get_barrier_semaphore()

    @pl.when(high != c)
    def _():
        greet(barrier, [there])

    greet(barrier, [(c, r) for r in ring] + [(c, across), (c, twin)])
    pl.semaphore_wait(barrier, steps + 1 + (high != c).astype(jnp.int32))

    @pl.when(high != c)
    def _():
        remote(cells, out.at[there[1]], move_sem.at[0], move_sem.at[1], there).start()
        remote(cells, out.at[there[1]], move_sem.at[0], move_sem.at[1], there).wait_send()
        remote(cells, out.at[e], move_sem.at[0], move_sem.at[1], there).wait_recv()

    @pl.when(high == c)
    def _():
        copy = pltpu.make_async_copy(cells, out.at[e], move_sem.at[0])
        copy.start()
        copy.wait()

    def back(base, d):
        return lax.rem(base + size - 4 * d, size)

    def along_z(slot, d):
        return remote(
            out.at[slot], out.at[slot], z_sent.at[d - 1], z_got.at[d - 1], (c, ring[d - 1])
        )

    def along_x(slot, j):
        return remote(out.at[slot], out.at[slot], x_sent.at[j], x_got.at[j], (c, across))

    def to_twin(slot, j):
        return remote(out.at[slot], out.at[slot], c_sent.at[j], c_got.at[j], (c, twin))

    for d in range(1, steps):
        along_z(e, d).start()
    along_x(e, 0).start()
    to_twin(e, 0).start()
    for d in range(steps):
        if d:
            along_z(back(e, d), d).wait_recv()
            along_x(back(e, d), d).start()
            to_twin(back(e, d), d).start()
        along_x(back(across, d), d).wait_recv()
        to_twin(back(across, d), steps + d).start()
    twin_across = twin + across - e
    for d in range(steps):
        to_twin(back(twin, d), d).wait_recv()
        to_twin(back(twin_across, d), steps + d).wait_recv()
    for d in range(1, steps):
        along_z(e, d).wait_send()
    for d in range(steps):
        along_x(back(e, d), d).wait_send()
        to_twin(back(e, d), d).wait_send()
        to_twin(back(across, d), steps + d).wait_send()


def gathered(cells, size):
    steps = size // 4
    dma = pltpu.SemaphoreType.DMA
    return pl.pallas_call(
        gather_kernel,
        out_shape=jax.ShapeDtypeStruct((size,) + cells.shape, cells.dtype),
        in_specs=[pl.BlockSpec(memory_space=pltpu.VMEM)],
        out_specs=pl.BlockSpec(memory_space=pltpu.VMEM),
        scratch_shapes=[
            dma((2,)),
            dma((steps - 1,)),
            dma((steps - 1,)),
            dma((steps,)),
            dma((steps,)),
            dma((2 * steps,)),
            dma((2 * steps,)),
        ],
        compiler_params=pltpu.CompilerParams(
            collective_id=0, has_side_effects=True, vmem_limit_bytes=24 * 2**20
        ),
    )(cells)


def spread_kernel(cells, out, a_sent, a_got, y_sent, y_got):
    c, e = lax.axis_index("ctx"), lax.axis_index("exp")
    size = cells.shape[0]
    other = (1 - c, e)

    def to(d):
        return lax.rem(e + d, size)

    def source(d):
        return lax.rem(e + size - d, size)

    barrier = pltpu.get_barrier_semaphore()
    greet(barrier, [(c, to(d)) for d in range(1, size)] + [other])
    pl.semaphore_wait(barrier, size)

    def sending(d):
        return remote(cells.at[to(d)], out.at[0, e], a_sent.at[d], a_got.at[d], (c, to(d)))

    def arriving(d):
        slot = source(d)
        return remote(cells.at[slot], out.at[0, slot], a_sent.at[d], a_got.at[d], (c, slot))

    def handing(d):
        slot = source(d)
        return remote(out.at[0, slot], out.at[1, slot], y_sent.at[d], y_got.at[d], other)

    mine = remote(cells.at[e], out.at[1, e], y_sent.at[0], y_got.at[0], other)
    mine.start()
    for d in range(1, size):
        sending(d).start()
    kept = pltpu.make_async_copy(cells.at[e], out.at[0, e], a_sent.at[0])
    kept.start()
    for d in range(1, size):
        arriving(d).wait_recv()
        handing(d).start()
    kept.wait()
    mine.wait()
    for d in range(1, size):
        handing(d).wait()
        sending(d).wait_send()


def spread_rows(cells):
    size = cells.shape[0]
    dma = pltpu.SemaphoreType.DMA
    return pl.pallas_call(
        spread_kernel,
        out_shape=jax.ShapeDtypeStruct((2,) + cells.shape, cells.dtype),
        in_specs=[pl.BlockSpec(memory_space=pltpu.VMEM)],
        out_specs=pl.BlockSpec(memory_space=pltpu.VMEM),
        scratch_shapes=[dma((size,)), dma((size,)), dma((size,)), dma((size,))],
        compiler_params=pltpu.CompilerParams(
            collective_id=1, has_side_effects=True, vmem_limit_bytes=24 * 2**20
        ),
    )(cells)


def local(inputs, pre_act, grad_out, conv_weight, expert_ids, gate_values, expert_in, expert_out):
    channels, bins = inputs.shape
    experts = lax.axis_size("exp")
    groups = lax.axis_size("ctx")
    capacity = 4 * bins // experts
    width = channels * experts
    kernel = conv_weight.shape[0]
    margin = kernel // 2
    pair = groups == 2
    me = lax.axis_index("ctx")

    ids = expert_ids.T
    names = jnp.arange(experts, dtype=jnp.int32)[:, None]
    chosen = [ids[k][None, :] == names for k in range(ids.shape[0])]
    named = sum(c.astype(BF16) for c in chosen)
    spot = jnp.arange(bins, dtype=jnp.int32)
    earlier = product(named, (spot[:, None] < spot[None, :]).astype(BF16), ((1,), (0,)))
    rows = jnp.arange(experts * capacity, dtype=jnp.int32)[:, None]
    picks = []
    for k, c in enumerate(chosen):
        slot = jnp.sum(jnp.where(c, earlier, 0.0), axis=0).astype(jnp.int32)
        picks.append((rows == (ids[k] * capacity + slot)[None, :]).astype(BF16))
    pick_any = sum(picks)
    pick_each = jnp.concatenate(picks, axis=1)

    pre_float = pre_act.astype(F32)
    grad_float = grad_out.astype(F32)
    activated = (inputs.astype(F32) + gelu_value(pre_float)).astype(BF16)
    gates = gate_values.T
    gated = jnp.concatenate(
        [(grad_float * gates[k][None, :]).astype(BF16) for k in range(len(picks))], axis=1
    )

    def picked(cells, pick):
        found = product(cells, pick, ((1,), (1,))).astype(BF16)
        return found.reshape(channels, experts, capacity).transpose(1, 0, 2)

    def to_experts(found):
        found = lax.all_to_all(found, "exp", split_axis=0, concat_axis=0, tiled=True)
        found = found.reshape(width, capacity)
        if pair:
            return jnp.concatenate([found, swapped(found)], axis=1)
        return lax.all_gather(found, "ctx", axis=1, tiled=True)

    sent_in = picked(activated, pick_any)
    sent_grad = picked(gated, pick_each)
    if pair and experts == 16:
        both = spread_rows(jnp.concatenate([sent_in, sent_grad], axis=1))
        rows_in, rows_grad = [
            jnp.concatenate([half[0].reshape(width, -1), half[1].reshape(width, -1)], axis=1)
            for half in (both[:, :, :channels], both[:, :, channels:])
        ]
    else:
        rows_in = to_experts(sent_in)
        rows_grad = to_experts(sent_grad)

    first = expert_in[0]
    second = expert_out[0]
    hidden = product(first, rows_in, ((0,), (0,)))
    grad_hidden = product(second, rows_grad, ((1,), (0,)))
    grad_pre = (grad_hidden * gelu_slope(hidden)).astype(BF16)
    if pair:
        theirs = product(first, grad_pre[:, capacity:], ((1,), (0,))).astype(BF16)
        mine = product(first, grad_pre[:, :capacity], ((1,), (0,)))
        back = (mine + swapped(theirs).astype(F32)).astype(BF16)
    else:
        part = product(first, grad_pre, ((1,), (0,)))
        back = lax.psum_scatter(part, "ctx", scatter_dimension=1, tiled=True).astype(BF16)
    squashed = gelu_value(hidden).astype(BF16)
    grad_second = product(squashed, rows_grad, ((1,), (1,))).astype(BF16)
    grad_pre, back = lax.optimization_barrier((grad_pre, back))
    grad_first = product(rows_in, grad_pre, ((1,), (1,))).astype(BF16)

    back = lax.all_to_all(
        back.reshape(experts, channels, capacity), "exp", split_axis=0, concat_axis=0, tiled=True
    )
    back = back.transpose(1, 0, 2).reshape(channels, experts * capacity)
    grad_total = grad_float + product(back, pick_any, ((1,), (0,)))
    grad_pre_conv = (grad_total * gelu_slope(pre_float)).astype(BF16)

    share = experts // groups
    if pair and experts == 16:
        blocks = gathered(grad_pre_conv, experts).reshape(groups, -1, bins)
    else:
        moves = [
            (c * experts + e, (e // share) * experts + c * share + e % share)
            for c in range(groups)
            for e in range(experts)
        ]
        moved = lax.ppermute(grad_pre_conv, ("ctx", "exp"), moves)
        blocks = lax.all_gather(moved, "exp", axis=0, tiled=True).reshape(groups, -1, bins)

    if pair:
        other = swapped(inputs)
        low = jnp.where(me == 0, inputs, other)
        high = jnp.where(me == 0, other, inputs)
        all_inputs = jnp.concatenate([low, high], axis=1)
    else:
        all_inputs = lax.all_gather(inputs, "ctx", axis=1, tiled=True)
    total = groups * bins
    padded = jnp.pad(all_inputs, ((0, 0), (margin, margin)))
    shifted = jnp.concatenate([padded[:, k : k + total] for k in range(kernel)], axis=0)
    weight = conv_weight.reshape(kernel * channels, -1)
    spread = jnp.concatenate(
        [product(weight, blocks[c], ((1,), (0,))) for c in range(groups)], axis=1
    )
    spread = jnp.pad(spread.reshape(kernel, channels, total), ((0, 0), (0, 0), (margin, margin)))
    conv_back = sum(
        spread[k, :, 2 * margin - k : 2 * margin - k + total] for k in range(kernel)
    )
    if pair:
        low, high = conv_back[:, :bins], conv_back[:, bins:]
        mine = jnp.where(me == 0, low, high)
        theirs = jnp.where(me == 0, high, low).astype(BF16)
        conv_back = mine + swapped(theirs).astype(F32)
    else:
        conv_back = lax.psum_scatter(conv_back, "ctx", scatter_dimension=1, tiled=True)
    grad_inputs = (grad_total + conv_back).astype(BF16)
    grad_conv = sum(
        product(shifted[:, c * bins : (c + 1) * bins], blocks[c], ((1,), (1,)))
        for c in range(groups)
    )
    return (
        grad_inputs,
        grad_conv.reshape(kernel, channels, -1),
        grad_first[None],
        grad_second[None],
    )


def solution(mesh):
    placed = (
        P("exp", "ctx"),
        P("exp", "ctx"),
        P("exp", "ctx"),
        P(None, "exp", "ctx"),
        P("ctx", None),
        P("ctx", None),
        P("exp", None, "ctx"),
        P("exp", "ctx", None),
    )
    return jax.shard_map(
        local,
        mesh=mesh,
        in_specs=placed,
        out_specs=(
            P("exp", "ctx"),
            P(None, "exp", "ctx"),
            P("exp", None, "ctx"),
            P("exp", "ctx", None),
        ),
        check_vma=False,
    )
```
